256 devices in a mesh: row: 8 (over z_hi, core), col: 32 (over x, y, z_lo).
Axes of the slice: x: 4, y: 4, z: 8 (z_hi: 4, z_lo: 2; z = z_hi * 2 + z_lo), core: 2. Of those that a mesh axis runs over, the one named last changes fastest.
Arguments:
- features: bfloat16 [32768, 128], P(('row', 'col')), may hold values from -6 to 6
- weight: bfloat16 [128, 512], replicated, may hold values from -0.5 to 0.5
- bias: float32 [512], replicated, may hold values from -4 to 4
- tile_values: bfloat16 [8, 32, 128, 128, 128], P('row', 'col'), may hold values from 0 to 0.019897461
- tile_index: int32 [8, 32, 128], P('row', 'col'), may hold values from 0 to 255, as said below
- tile_count: int32 [8, 32], P('row', 'col'), may hold values from 16 to 128, as said below
- cotangent: bfloat16 [32768, 512], P(('col', 'row')), may hold values from -20 to 20
Outputs:
- hidden_out: bfloat16 [32768, 512], P(('col', 'row'))
- grad_features: bfloat16 [32768, 128], P(('row', 'col'))
- grad_weight: float32 [128, 512], replicated
- grad_bias: float32 [512], replicated
The draws below stay inside these ranges and needn't reach their ends.
Inputs may be any that keep to these rules, and one draw needn't show every extreme that they name: `tile_index`: within a cell the slots name distinct tiles; slots at or beyond the cell's count hold arbitrary tiles and values. `tile_count`: counts differ from cell to cell; some cell holds exactly 128 live slots.
All inputs are finite; a program needn't handle non-finite values.
Results may differ from the reference program's by a relative error of at most 0.0065.
Values may be sent and summed in bfloat16 or wider, within the bound.
No kernel may reach another device: no remote copies, remote signals or barrier semaphores. Data moves between devices by JAX's collectives and lax.ppermute only.
A program may use at most 128 MiB of HBM per device.

```python
import jax
import jax.numpy as jnp
from jax import lax

F = 128
HID = 512
TILE = 128
NODES = 32768
TR = 8
TC = 32
KMAX = 128
N_ROW = 8
N_COL = 32


def draw_tile_index(key, part):
    key = jax.random.fold_in(key, 1)
    keys = jax.random.split(key, N_ROW * N_COL)
    places = jax.vmap(lambda k: jax.random.permutation(k, TR * TC)[:KMAX])(keys)
    return places.reshape(N_ROW, N_COL, KMAX).astype(jnp.int32)


def draw_tile_count(key, part):
    key = jax.random.fold_in(key, 2)
    key_one, key_two, key_three = jax.random.split(key, 3)
    lowest = max(1, KMAX // 8)
    first = jax.random.randint(key_one, (N_ROW * N_COL,), lowest, KMAX + 1)
    second = jax.random.randint(key_two, (N_ROW * N_COL,), lowest, KMAX + 1)
    counts = jnp.minimum(first, second)
    fullest = jax.random.randint(key_three, (), 0, N_ROW * N_COL)
    counts = counts.at[fullest].set(KMAX)
    return counts.reshape(N_ROW, N_COL).astype(jnp.int32)


def draw_cotangent(key, part):
    key = jax.random.fold_in(key, 3)
    place = jnp.arange(NODES, dtype=jnp.float32)[:, None] / NODES
    scale = 3.0 ** place
    values = jnp.clip(jax.random.normal(key, (NODES, HID), jnp.float32), -4.0, 4.0) * scale
    return values.astype(jnp.bfloat16)


def shard_levels(own_key, extent, pieces, smallest, high):
    level, own = 1.0, jax.random.fold_in(own_key, 6)
    for dim, blocks in pieces:
        steps = jnp.exp(jax.random.uniform(jax.random.fold_in(own, dim), (blocks,), jnp.float32, smallest / len(pieces), high / len(pieces)))
        level = level * jnp.repeat(steps, extent[dim] // blocks).reshape([-1 if axis == dim else 1 for axis in range(len(extent))])
    return level


def centred(key, extent, deviation, most, cuts=(), kind=jnp.bfloat16):
    values = deviation * jax.random.normal(key, extent, jnp.float32)
    if cuts:
        values = values * shard_levels(key, extent, cuts, -0.22, 0.18)
    return jnp.clip(values, -most, most).astype(kind)


def setup_inputs(seed: int = 0) -> dict:
    key_list = jax.random.split(jax.random.key(seed), 8)
    return {
        "features": centred(key_list[0], (NODES, F), 1.0, 6.0, ((0, 256),)),
        "weight": centred(key_list[1], (F, HID), F ** -0.5, 0.5),
        "bias": centred(key_list[2], (HID,), 1.0, 4.0, (), jnp.float32),
        "tile_values": jnp.clip(0.019897461 * jax.random.uniform(key_list[3], (N_ROW, N_COL, KMAX, TILE, TILE), jnp.float32) ** shard_levels(key_list[3], (N_ROW, N_COL, KMAX, TILE, TILE), ((0, 8), (1, 32)), -0.2, 0.2), 0.0, 0.019897461).astype(jnp.bfloat16),
        "tile_index": draw_tile_index(jax.random.fold_in(key_list[7], 71), 0),
        "tile_count": draw_tile_count(jax.random.fold_in(key_list[7], 71), 0),
        "cotangent": draw_cotangent(jax.random.fold_in(key_list[7], 71), 0),
    }


def tile_products(tiles, take_idx, put_idx, live, source, count_out, backward):
    picked = jnp.take(source, take_idx, axis=0)
    if backward:
        prod = jnp.einsum("kab,kah->kbh", tiles.astype(jnp.float32), picked.astype(jnp.float32), precision=lax.Precision.HIGHEST)
    else:
        prod = jnp.einsum("kab,kbh->kah", tiles.astype(jnp.float32), picked.astype(jnp.float32), precision=lax.Precision.HIGHEST)
    onehot = ((put_idx[None, :] == jnp.arange(count_out, dtype=jnp.int32)[:, None]) & live[None, :]).astype(jnp.float32)
    return jnp.einsum("tk,kah->tah", onehot, prod, precision=lax.Precision.HIGHEST)


def reference(features, weight, bias, tile_values, tile_index, tile_count, cotangent):
    projected = jnp.dot(features, weight, preferred_element_type=jnp.float32)
    source_rows = TC * TILE
    target_rows = TR * TILE
    slots = jnp.arange(KMAX, dtype=jnp.int32)

    def forward_col(c):
        def add(r, acc):
            idx = tile_index[r, c]
            live = slots < tile_count[r, c]
            block = lax.dynamic_slice_in_dim(projected, (r * source_rows).astype(jnp.int32), source_rows, 0)
            block = block.reshape(TC, TILE, HID)
            return acc + tile_products(tile_values[r, c], idx % TC, idx // TC, live, block, TR, False)
        return lax.fori_loop(0, N_ROW, add, jnp.zeros((TR, TILE, HID), jnp.float32))

    pre = lax.map(forward_col, jnp.arange(N_COL, dtype=jnp.int32)).reshape(NODES, HID) + bias[None, :]
    hidden_out = jax.nn.silu(pre).astype(jnp.bfloat16)
    sig = jax.nn.sigmoid(pre)
    dpre = (cotangent.astype(jnp.float32) * (sig + pre * sig * (1.0 - sig))).astype(jnp.bfloat16)
    grad_bias = jnp.sum(dpre.astype(jnp.float32), axis=0)

    def backward_row(r):
        def add(c, acc):
            idx = tile_index[r, c]
            live = slots < tile_count[r, c]
            block = lax.dynamic_slice_in_dim(dpre, (c * target_rows).astype(jnp.int32), target_rows, 0)
            block = block.reshape(TR, TILE, HID)
            return acc + tile_products(tile_values[r, c], idx // TC, idx % TC, live, block, TC, True)
        return lax.fori_loop(0, N_COL, add, jnp.zeros((TC, TILE, HID), jnp.float32))

    dproj = lax.map(backward_row, jnp.arange(N_ROW, dtype=jnp.int32)).reshape(NODES, HID)
    grad_features = jnp.dot(dproj, weight.astype(jnp.float32).T, precision=lax.Precision.HIGHEST).astype(jnp.bfloat16)
    grad_weight = jnp.dot(features.astype(jnp.float32).T, dproj, precision=lax.Precision.HIGHEST)
    return hidden_out, grad_features, grad_weight, grad_bias
```

```python
import jax
import jax.numpy as jnp
from jax import lax
from jax.experimental import pallas as pl
from jax.experimental.pallas import tpu as pltpu
from jax.sharding import PartitionSpec as P

BF, F32 = jnp.bfloat16, jnp.float32
VMEM = pltpu.VMEM


def ring(count, inner, size, step):
    pairs = []
    for i in range(size):
        digit = (i // inner) % count
        pairs.append((i, i + (((digit + step) % count) - digit) * inner))
    return pairs


def move_x(v, step):
    return lax.ppermute(v, "col", ring(4, 8, 32, step))


def move_y(v, step):
    return lax.ppermute(v, "col", ring(4, 2, 32, step))


def move_z(v):
    return lax.ppermute(v, "col", ring(2, 1, 32, 1))


def move_h(v, step):
    return lax.ppermute(v, "row", ring(4, 2, 8, step))


def move_k(v):
    return lax.ppermute(v, "row", ring(2, 1, 8, 1))


def spread_kernel(count_ref, put_row, put_col, tiles_ref, dense_ref):
    size = tiles_ref.shape[1]
    dense_ref[...] = jnp.zeros_like(dense_ref)

    def place(slot, carry):
        rows = pl.ds(pl.multiple_of(put_row[slot] * size, size), size)
        cols = pl.ds(pl.multiple_of(put_col[slot] * size, size), size)
        dense_ref[rows, cols] = tiles_ref[slot]
        return carry

    lax.fori_loop(0, count_ref[0], place, 0)


def spread(tiles, count, put_row, put_col, rows, cols):
    slots, size, _ = tiles.shape
    smem = pl.BlockSpec(memory_space=pltpu.SMEM)
    return pl.pallas_call(
        spread_kernel,
        out_shape=jax.ShapeDtypeStruct((rows * size, cols * size), BF),
        in_specs=[smem, smem, smem, pl.BlockSpec(memory_space=VMEM)],
        out_specs=pl.BlockSpec(memory_space=VMEM),
        compiler_params=pltpu.CompilerParams(vmem_limit_bytes=32 * 2**20),
        cost_estimate=pl.CostEstimate(
            flops=0, bytes_accessed=2 * size * size * (slots + rows * cols), transcendentals=0
        ),
        name="spread",
    )(count, put_row, put_col, tiles)


def middle_kernel(
    place, own, in1, in2, in3, weight, bias, cot, hidden_ref, back_ref, gw_ref, whole
):
    agg = own[...] + in1[...].astype(F32) + in2[...].astype(F32) + in3[...].astype(F32)
    high = agg.astype(BF)
    low = (agg - high.astype(F32)).astype(BF)
    w = weight[...]
    pre = (
        jnp.dot(high, w, preferred_element_type=F32)
        + jnp.dot(low, w, preferred_element_type=F32)
        + bias[...]
    )
    sig = jax.nn.sigmoid(pre)
    hidden_ref[...] = (pre * sig).astype(BF)
    dpre = (cot[...].astype(F32) * (sig + pre * sig * (1.0 - sig))).astype(BF)
    back_ref[...] = lax.dot_general(
        dpre, w, (((1,), (1,)), ((), ())), preferred_element_type=F32
    ).astype(BF)
    over_nodes = (((0,), (0,)), ((), ()))
    whole[...] = lax.dot_general(
        high, dpre, over_nodes, preferred_element_type=F32
    ) + lax.dot_general(low, dpre, over_nodes, preferred_element_type=F32)
    sums = jnp.sum(dpre.astype(F32), axis=0, keepdims=True)
    nh, nk, rows, _ = gw_ref.shape
    wide = weight.shape[1]
    for h in range(nh):
        for k in range(nk):
            at = (lax.rem(place[0] - h + nh, nh) * nk + lax.rem(place[1] + k, nk)) * rows
            gw_ref[h, k, :, :wide] = whole[pl.ds(pl.multiple_of(at, rows), rows), :]
            gw_ref[h, k, :, wide:] = jnp.zeros((rows, 128), F32)
    for h in range(nh):
        for k in range(nk):
            for j in range(wide // 128):
                gw_ref[h, k, j : j + 1, wide:] = sums[:, j * 128 : (j + 1) * 128]


def middle(place, own, arrived, weight, bias, cotangent):
    size, width = cotangent.shape
    feats = weight.shape[0]
    vmem = pl.BlockSpec(memory_space=VMEM)
    return pl.pallas_call(
        middle_kernel,
        out_shape=(
            jax.ShapeDtypeStruct((size, width), BF),
            jax.ShapeDtypeStruct((size, feats), BF),
            jax.ShapeDtypeStruct((4, 2, feats // 8, width + 128), F32),
        ),
        in_specs=[pl.BlockSpec(memory_space=pltpu.SMEM)] + [vmem] * 7,
        out_specs=(vmem, vmem, vmem),
        scratch_shapes=[VMEM((feats, width), F32)],
        compiler_params=pltpu.CompilerParams(vmem_limit_bytes=16 * 2**20),
        cost_estimate=pl.CostEstimate(
            flops=10 * size * feats * width, bytes_accessed=10 * size * width, transcendentals=size * width
        ),
        name="middle",
    )(place, own, *arrived, weight, bias[None, :], cotangent)


def settle_kernel(place, parts, out_ref, bias_ref):
    nk, nh, rows, _ = parts.shape
    wide = out_ref.shape[1]
    for h in range(nh):
        for k in range(nk):
            at = (lax.rem(place[0] - h + nh, nh) * nk + lax.rem(place[1] + k, nk)) * rows
            out_ref[pl.ds(pl.multiple_of(at, rows), rows), :] = parts[k, h, :, :wide]
    bias_ref[...] = parts[0, 0, :8, wide:]


def settle(place, parts):
    nk, nh, rows, width = parts.shape
    vmem = pl.BlockSpec(memory_space=VMEM)
    return pl.pallas_call(
        settle_kernel,
        out_shape=(
            jax.ShapeDtypeStruct((nk * nh * rows, width - 128), F32),
            jax.ShapeDtypeStruct((8, 128), F32),
        ),
        in_specs=[pl.BlockSpec(memory_space=pltpu.SMEM), vmem],
        out_specs=(vmem, vmem),
        name="settle",
    )(place, parts)


def local(features, weight, bias, tile_values, tile_index, tile_count, cotangent):
    size = features.shape[0]
    feats, width = weight.shape
    places = tile_index[0, 0]
    row, col = lax.axis_index("row"), lax.axis_index("col")
    h, k = row // 2, row % 2
    x, y, z = col // 8, (col // 2) % 4, col % 2
    here = jnp.stack([h, k]).astype(jnp.int32)

    tile_row, tile_col = places // 32, places % 32
    far_h, far_k = (h - tile_row // 2) % 4, (k - tile_row) % 2
    far_x, far_y, far_z = (x - tile_col // 8) % 4, (y - tile_col // 2) % 4, (z - tile_col) % 2
    put_row = (far_k * 4 + far_h).astype(jnp.int32)
    put_col = jnp.where(far_z == 0, far_x * 4 + far_y, 16 + far_y * 4 + far_x).astype(jnp.int32)
    dense = spread(tile_values[0, 0], tile_count[0], put_row, put_col, 8, 32)

    near, other = features, move_z(features)
    near = jnp.stack([near] + [move_y(near, s) for s in (1, 2, 3)])
    other = jnp.stack([other] + [move_x(other, s) for s in (1, 2, 3)])
    near = jnp.stack([near] + [move_x(near, s) for s in (1, 2, 3)])
    other = jnp.stack([other] + [move_y(other, s) for s in (1, 2, 3)])
    source = jnp.concatenate([near.reshape(-1, feats), other.reshape(-1, feats)])

    part = jnp.dot(dense, source, preferred_element_type=F32).reshape(2, 4, size, feats)
    half = part[0] + move_k(part[1].astype(BF)).astype(F32)
    sent = half.astype(BF)
    arrived = [move_h(sent[s], -s) for s in (1, 2, 3)]
    hidden_out, back, gw = middle(here, half[0], arrived, weight, bias, cotangent)

    target = jnp.stack([back] + [move_h(back, s) for s in (1, 2, 3)])
    target = jnp.stack([target, move_k(target)]).reshape(-1, feats)
    grad = lax.dot_general(dense, target, (((0,), (0,)), ((), ())), preferred_element_type=F32)
    grad = grad.reshape(2, 4, 4, size, feats)
    near, other = grad[0], grad[1]

    def fold(parts, move):
        low = parts.astype(BF)
        return parts[0] + sum(move(low[s], -s).astype(F32) for s in (1, 2, 3))

    near = fold(fold(near, move_x), move_y)
    other = fold(fold(other, move_y), move_x)
    grad_features = (near + move_z(other.astype(BF)).astype(F32)).astype(BF)

    gw = gw[0] + sum(move_h(gw[s], -s) for s in (1, 2, 3))
    gw = gw[0] + move_k(gw[1])
    gw = gw + move_z(gw)
    gw = gw + sum(move_y(gw, s) for s in (1, 2, 3))
    gw = gw + sum(move_x(gw, s) for s in (1, 2, 3))
    gw = jnp.stack([gw] + [move_h(gw, s) for s in (1, 2, 3)])
    gw = jnp.stack([gw, move_k(gw)])
    grad_weight, sums = settle(here, gw)
    grad_bias = sums[: width // 128].reshape(width)
    return (hidden_out, grad_features, grad_weight, grad_bias)


def solution(mesh):
    in_specs = (
        P(("row", "col"), None),
        P(),
        P(),
        P("row", "col", None, None, None),
        P("row", "col", None),
        P("row", "col"),
        P(("col", "row"), None),
    )
    out_specs = (P(("col", "row"), None), P(("row", "col"), None), P(), P())
    return jax.shard_map(local, mesh=mesh, in_specs=in_specs, out_specs=out_specs, check_vma=False)
```

```python
import jax
import jax.numpy as jnp
from jax import lax
from jax.experimental import pallas as pl
from jax.experimental.pallas import tpu as pltpu
from jax.sharding import PartitionSpec as P

BF, F32 = jnp.bfloat16, jnp.float32
VMEM = pltpu.VMEM


def ring(count, inner, size, step):
    pairs = []
    for i in range(size):
        digit = (i // inner) % count
        pairs.append((i, i + (((digit + step) % count) - digit) * inner))
    return pairs


def mirror(count, inner, size, mask):
    pairs = []
    for i in range(size):
        digit = (i // inner) % count
        pairs.append((i, i + ((digit ^ mask) - digit) * inner))
    return pairs


def move_x(v, step):
    return lax.ppermute(v, "col", ring(4, 8, 32, step))


def move_y(v, step):
    return lax.ppermute(v, "col", ring(4, 2, 32, step))


def move_h(v, step):
    return lax.ppermute(v, "row", ring(4, 2, 8, step))


def swap_x(v, mask):
    return lax.ppermute(v, "col", mirror(4, 8, 32, mask))


def swap_y(v, mask):
    return lax.ppermute(v, "col", mirror(4, 2, 32, mask))


def swap_z(v):
    return lax.ppermute(v, "col", mirror(2, 1, 32, 1))


def swap_k(v):
    return lax.ppermute(v, "row", mirror(2, 1, 8, 1))


def pair(v):
    high = v.astype(BF)
    return jnp.concatenate([high, (v - high.astype(F32)).astype(BF)])


def unpair(v):
    rows = v.shape[0] // 2
    return v[:rows].astype(F32) + v[rows:].astype(F32)


def spread_kernel(count_ref, put_row, put_col, tiles_ref, dense_ref, sems):
    size = tiles_ref.shape[1]
    dense_ref[...] = jnp.zeros_like(dense_ref)

    def copy(slot):
        rows = pl.ds(pl.multiple_of(put_row[slot] * size, size), size)
        cols = pl.ds(pl.multiple_of(put_col[slot] * size, size), size)
        return pltpu.make_async_copy(tiles_ref.at[slot], dense_ref.at[rows, cols], sems.at[slot])

    def begin(slot, carry):
        copy(slot).start()
        return carry

    def end(slot, carry):
        copy(slot).wait()
        return carry

    lax.fori_loop(0, count_ref[0], begin, 0)
    lax.fori_loop(0, count_ref[0], end, 0)


def spread(tiles, count, put_row, put_col, rows, cols):
    slots, size, _ = tiles.shape
    smem = pl.BlockSpec(memory_space=pltpu.SMEM)
    return pl.pallas_call(
        spread_kernel,
        out_shape=jax.ShapeDtypeStruct((rows * size, cols * size), BF),
        in_specs=[smem, smem, smem, pl.BlockSpec(memory_space=pl.ANY)],
        out_specs=pl.BlockSpec(memory_space=VMEM),
        scratch_shapes=[pltpu.SemaphoreType.DMA((slots,))],
        compiler_params=pltpu.CompilerParams(vmem_limit_bytes=32 * 2**20),
        cost_estimate=pl.CostEstimate(
            flops=0, bytes_accessed=2 * size * size * (slots + rows * cols), transcendentals=0
        ),
        name="spread",
    )(count, put_row, put_col, tiles)


def middle_kernel(place, own, in1, in2, in3, weight, bias, cot, hidden_ref, sent_ref, gw_ref, whole):
    agg = own[...] + in1[...].astype(F32) + in2[...].astype(F32) + in3[...].astype(F32)
    high = agg.astype(BF)
    low = (agg - high.astype(F32)).astype(BF)
    w = weight[...]
    pre = (
        jnp.dot(high, w, preferred_element_type=F32)
        + jnp.dot(low, w, preferred_element_type=F32)
        + bias[...]
    )
    sig = jax.nn.sigmoid(pre)
    hidden_ref[...] = (pre * sig).astype(BF)
    dpre = (cot[...].astype(F32) * (sig + pre * sig * (1.0 - sig))).astype(BF)
    back = lax.dot_general(
        dpre, w, (((1,), (1,)), ((), ())), preferred_element_type=F32
    ).astype(BF)
    over_nodes = (((0,), (0,)), ((), ()))
    whole[...] = lax.dot_general(
        high, dpre, over_nodes, preferred_element_type=F32
    ) + lax.dot_general(low, dpre, over_nodes, preferred_element_type=F32)
    sums = jnp.sum(dpre.astype(F32), axis=0, keepdims=True)
    size, lanes = back.shape
    blocks = cot.shape[1] // lanes
    rows = whole.shape[0] // 8
    tail = jnp.concatenate(
        [sums[:, j * lanes : (j + 1) * lanes] for j in range(blocks)]
        + [jnp.zeros((rows - blocks, lanes), F32)]
    )
    for h in range(4):
        sent_ref[h, :size, :] = back
        for k in range(2):
            at = (lax.rem(place[0] + h, 4) * 2 + lax.rem(place[1] + k, 2)) * rows
            for j in range(blocks + 1):
                if j < blocks:
                    piece = whole[pl.ds(pl.multiple_of(at, rows), rows), j * lanes : (j + 1) * lanes]
                else:
                    piece = tail
                to = (k * (blocks + 1) + j) * rows
                sent_ref[h, size + to : size + to + rows, :] = piece.astype(BF)
                if h == 0:
                    gw_ref[to : to + rows, :] = piece


def middle(place, own, arrived, weight, bias, cotangent):
    size, width = cotangent.shape
    feats = weight.shape[0]
    share = 2 * (feats // 8) * (width // feats + 1)
    vmem = pl.BlockSpec(memory_space=VMEM)
    return pl.pallas_call(
        middle_kernel,
        out_shape=(
            jax.ShapeDtypeStruct((size, width), BF),
            jax.ShapeDtypeStruct((4, size + share, feats), BF),
            jax.ShapeDtypeStruct((share, feats), F32),
        ),
        in_specs=[pl.BlockSpec(memory_space=pltpu.SMEM)] + [vmem] * 7,
        out_specs=(vmem, vmem, vmem),
        scratch_shapes=[VMEM((feats, width), F32)],
        compiler_params=pltpu.CompilerParams(vmem_limit_bytes=16 * 2**20),
        cost_estimate=pl.CostEstimate(
            flops=10 * size * feats * width, bytes_accessed=10 * size * width, transcendentals=size * width
        ),
        name="middle",
    )(place, own, *arrived, weight, bias[None, :], cotangent)


def settle_kernel(place, near, far, out_ref, bias_ref):
    lanes = near.shape[1]
    blocks = out_ref.shape[1] // lanes
    rows = near.shape[0] // 4 // (blocks + 1)
    for k in range(2):
        part = far if k else near
        for h in range(4):
            at = (lax.rem(place[0] - h + 4, 4) * 2 + lax.rem(place[1] + k, 2)) * rows
            for j in range(blocks):
                first = (h * (blocks + 1) + j) * rows
                out_ref[pl.ds(pl.multiple_of(at, rows), rows), j * lanes : (j + 1) * lanes] = part[
                    first : first + rows, :
                ]
    for j in range(blocks):
        bias_ref[:, j * lanes : (j + 1) * lanes] = near[blocks * rows + j : blocks * rows + j + 1, :]


def settle(place, near, far, feats, width):
    vmem = pl.BlockSpec(memory_space=VMEM)
    return pl.pallas_call(
        settle_kernel,
        out_shape=(
            jax.ShapeDtypeStruct((feats, width), F32),
            jax.ShapeDtypeStruct((1, width), F32),
        ),
        in_specs=[pl.BlockSpec(memory_space=pltpu.SMEM), vmem, vmem],
        out_specs=(vmem, vmem),
        name="settle",
    )(place, near, far)


def local(features, weight, bias, tile_values, tile_index, tile_count, cotangent):
    size = features.shape[0]
    feats, width = weight.shape
    places = tile_index[0, 0]
    row, col = lax.axis_index("row"), lax.axis_index("col")
    h, k = row // 2, row % 2
    x, y, z = col // 8, (col // 2) % 4, col % 2
    here = jnp.stack([h, k]).astype(jnp.int32)

    tile_row, tile_col = places // 32, places % 32
    from_x, from_y = tile_col // 8, (tile_col // 2) % 4
    far_h, far_k = (h - tile_row // 2) % 4, (k - tile_row) % 2
    bits_x, bits_y = x ^ from_x, y ^ from_y
    put_row = (far_k * 4 + far_h).astype(jnp.int32)
    put_col = jnp.where(
        (z - tile_col) % 2 == 0,
        ((x - from_x) % 4) * 4 + (bits_y ^ (bits_y >> 1)),
        16 + ((y - from_y) % 4) * 4 + (bits_x ^ (bits_x >> 1)),
    ).astype(jnp.int32)
    dense = spread(tile_values[0, 0], tile_count[0], put_row, put_col, 8, 32)

    near, other = features, swap_z(features)
    near = jnp.concatenate([near, swap_y(near, 1)])
    other = jnp.concatenate([other, swap_x(other, 1)])
    near = jnp.concatenate([near, swap_y(near, 3)])
    other = jnp.concatenate([other, swap_x(other, 3)])
    near = [near] + [move_x(near, s) for s in (1, 2, 3)]
    other = [other] + [move_y(other, s) for s in (1, 2, 3)]
    source = jnp.concatenate(near + other)

    part = jnp.dot(dense, source, preferred_element_type=F32).reshape(2, 4, size, feats)
    half = part[0] + swap_k(part[1].astype(BF)).astype(F32)
    sent = half.astype(BF)
    arrived = [move_h(sent[s], -s) for s in (1, 2, 3)]
    hidden_out, sent, gw = middle(here, half[0], arrived, weight, bias, cotangent)

    arrived = [move_h(sent[s], s) for s in (1, 2, 3)]
    target = jnp.concatenate([sent[0][:size]] + [v[:size] for v in arrived])
    gw = gw + sum(v[size:].astype(F32) for v in arrived)
    share = gw.shape[0] // 2
    arrived = swap_k(jnp.concatenate([target, pair(gw[share:])]))
    gw = pair(gw[:share] + unpair(arrived[4 * size :]))
    target = jnp.concatenate([target, arrived[: 4 * size]])
    grad = lax.dot_general(dense, target, (((0,), (0,)), ((), ())), preferred_element_type=F32)
    grad = grad.reshape(2, 4, 4 * size, feats)
    near, other = grad[0], grad[1]

    rows = 4 * size
    arrived = [move_x(jnp.concatenate([near[s].astype(BF), gw]), -s) for s in (1, 2, 3)]
    near = near[0] + sum(v[:rows].astype(F32) for v in arrived)
    one, two, three = [unpair(v[rows:]) for v in arrived]
    gw = pair((unpair(gw) + two) + (one + three))
    other = other[0] + sum(move_y(other[s].astype(BF), -s).astype(F32) for s in (1, 2, 3))
    for mask in (3, 1):
        rows = rows // 2
        arrived = swap_y(jnp.concatenate([near[rows:].astype(BF), gw]), mask)
        near = near[:rows] + arrived[:rows].astype(F32)
        gw = pair(unpair(gw) + unpair(arrived[rows:]))
        other = other[:rows] + swap_x(other[rows:].astype(BF), mask).astype(F32)
    arrived = swap_z(jnp.concatenate([other.astype(BF), gw]))
    grad_features = (near + arrived[:rows].astype(F32)).astype(BF)
    gw = unpair(gw) + unpair(arrived[rows:])

    gw = jnp.concatenate([gw] + [move_h(gw, s) for s in (1, 2, 3)])
    grad_weight, grad_bias = settle(here, gw, swap_k(gw), feats, width)
    return (hidden_out, grad_features, grad_weight, grad_bias.reshape(width))


def solution(mesh):
    in_specs = (
        P(("row", "col"), None),
        P(),
        P(),
        P("row", "col", None, None, None),
        P("row", "col", None),
        P("row", "col"),
        P(("col", "row"), None),
    )
    out_specs = (P(("col", "row"), None), P(("row", "col"), None), P(), P())
    return jax.shard_map(local, mesh=mesh, in_specs=in_specs, out_specs=out_specs, check_vma=False)
```

```python
import jax
import jax.numpy as jnp
from jax import lax
from jax.experimental import pallas as pl
from jax.experimental.pallas import tpu as pltpu
from jax.sharding import PartitionSpec as P

BF, F32 = jnp.bfloat16, jnp.float32
VMEM = pltpu.VMEM


def ring(i, count, inner, step):
    digit = (i // inner) % count
    return i + ((digit + step) % count - digit) * inner


def mirror(i, count, inner, mask):
    digit = (i // inner) % count
    return i + ((digit ^ mask) - digit) * inner


def move_xy(v, step, turn):
    pairs = []
    for i in range(256):
        row, col = i // 32, i % 32
        pairs.append((i, row * 32 + ring(col, 4, 2 if row % 2 == turn else 8, step)))
    return lax.ppermute(v, ("row", "col"), pairs)


def move_h(v, step):
    return lax.ppermute(v, "row", [(i, ring(i, 4, 2, step)) for i in range(8)])


def swap_h(v, mask):
    return lax.ppermute(v, "row", [(i, mirror(i, 4, 2, mask)) for i in range(8)])


def swap_k(v):
    return lax.ppermute(v, "row", [(i, i ^ 1) for i in range(8)])


def swap_z(v):
    return lax.ppermute(v, "col", [(i, i ^ 1) for i in range(32)])


def pair(v):
    high = v.astype(BF)
    return jnp.concatenate([high, (v - high.astype(F32)).astype(BF)])


def unpair(v):
    rows = v.shape[0] // 2
    return v[:rows].astype(F32) + v[rows:].astype(F32)


def spread_kernel(count_ref, put_row, put_col, tiles_ref, dense_ref):
    size = tiles_ref.shape[1]
    dense_ref[...] = jnp.zeros_like(dense_ref)

    def place(slot, carry):
        rows = pl.ds(pl.multiple_of(put_row[slot] * size, size), size)
        cols = pl.ds(pl.multiple_of(put_col[slot] * size, size), size)
        dense_ref[rows, cols] = tiles_ref[slot]
        return carry

    lax.fori_loop(0, count_ref[0], place, 0)


def spread(tiles, count, put_row, put_col, rows, cols):
    slots, size, _ = tiles.shape
    smem = pl.BlockSpec(memory_space=pltpu.SMEM)
    return pl.pallas_call(
        spread_kernel,
        out_shape=jax.ShapeDtypeStruct((rows * size, cols * size), BF),
        in_specs=[smem, smem, smem, pl.BlockSpec(memory_space=VMEM)],
        out_specs=pl.BlockSpec(memory_space=VMEM),
        compiler_params=pltpu.CompilerParams(vmem_limit_bytes=32 * 2**20),
        cost_estimate=pl.CostEstimate(
            flops=0, bytes_accessed=2 * size * size * (slots + rows * cols), transcendentals=0
        ),
        name="spread",
    )(count, put_row, put_col, tiles)


def middle_kernel(place, own, in1, in2, in3, weight, bias, cot, hidden_ref, sent_ref, gw_ref, whole):
    agg = own[...] + in1[...].astype(F32) + in2[...].astype(F32) + in3[...].astype(F32)
    high = agg.astype(BF)
    low = (agg - high.astype(F32)).astype(BF)
    w = weight[...]
    pre = (
        jnp.dot(high, w, preferred_element_type=F32)
        + jnp.dot(low, w, preferred_element_type=F32)
        + bias[...]
    )
    sig = jax.nn.sigmoid(pre)
    hidden_ref[...] = (pre * sig).astype(BF)
    dpre = (cot[...].astype(F32) * (sig + pre * sig * (1.0 - sig))).astype(BF)
    back = lax.dot_general(
        dpre, w, (((1,), (1,)), ((), ())), preferred_element_type=F32
    ).astype(BF)
    over_nodes = (((0,), (0,)), ((), ()))
    whole[...] = lax.dot_general(
        high, dpre, over_nodes, preferred_element_type=F32
    ) + lax.dot_general(low, dpre, over_nodes, preferred_element_type=F32)
    sums = jnp.sum(dpre.astype(F32), axis=0, keepdims=True)
    size, lanes = back.shape
    blocks = cot.shape[1] // lanes
    rows = whole.shape[0] // 8
    tail = jnp.concatenate(
        [sums[:, j * lanes : (j + 1) * lanes] for j in range(blocks)]
        + [jnp.zeros((rows - blocks, lanes), F32)]
    )
    for h in range(4):
        sent_ref[h, :size, :] = back
        for k in range(2):
            at = (lax.rem(place[0] + h, 4) * 2 + (place[1] ^ k)) * rows
            at = pl.ds(pl.multiple_of(at, rows), rows)
            for j in range(blocks + 1):
                piece = whole[at, j * lanes : (j + 1) * lanes] if j < blocks else tail
                to = (k * (blocks + 1) + j) * rows
                sent_ref[h, size + to : size + to + rows, :] = piece.astype(BF)
                if h == 0:
                    gw_ref[to : to + rows, :] = piece


def middle(place, own, arrived, weight, bias, cotangent):
    size, width = cotangent.shape
    feats = weight.shape[0]
    share = (feats // 4) * (width // feats + 1)
    vmem = pl.BlockSpec(memory_space=VMEM)
    return pl.pallas_call(
        middle_kernel,
        out_shape=(
            jax.ShapeDtypeStruct((size, width), BF),
            jax.ShapeDtypeStruct((4, size + share, feats), BF),
            jax.ShapeDtypeStruct((share, feats), F32),
        ),
        in_specs=[pl.BlockSpec(memory_space=pltpu.SMEM)] + [vmem] * 7,
        out_specs=(vmem, vmem, vmem),
        scratch_shapes=[VMEM((feats, width), F32)],
        compiler_params=pltpu.CompilerParams(vmem_limit_bytes=16 * 2**20),
        cost_estimate=pl.CostEstimate(
            flops=10 * size * feats * width, bytes_accessed=10 * size * width, transcendentals=size * width
        ),
        name="middle",
    )(place, own, *arrived, weight, bias[None, :], cotangent)


def settle_kernel(place, near, far, out_ref):
    lanes = near.shape[1]
    blocks = out_ref.shape[1] // lanes
    rows = near.shape[0] // 4 // blocks
    for k, part in ((0, near), (1, far)):
        for first, bits in enumerate((0, 1, 3, 2)):
            at = ((place[0] ^ bits) * 2 + (place[1] ^ k)) * rows
            at = pl.ds(pl.multiple_of(at, rows), rows)
            for j in range(blocks):
                start = (first * blocks + j) * rows
                out_ref[at, j * lanes : (j + 1) * lanes] = part[start : start + rows, :].astype(F32)


def settle(place, near, far, feats, width):
    vmem = pl.BlockSpec(memory_space=VMEM)
    return pl.pallas_call(
        settle_kernel,
        out_shape=jax.ShapeDtypeStruct((feats, width), F32),
        in_specs=[pl.BlockSpec(memory_space=pltpu.SMEM), vmem, vmem],
        out_specs=vmem,
        compiler_params=pltpu.CompilerParams(vmem_limit_bytes=16 * 2**20),
        name="settle",
    )(place, near, far)


def local(features, weight, bias, tile_values, tile_index, tile_count, cotangent):
    size = features.shape[0]
    feats, width = weight.shape
    places = tile_index[0, 0]
    row, col = lax.axis_index("row"), lax.axis_index("col")
    h, k = row // 2, row % 2
    x, y, z = col // 8, (col // 2) % 4, col % 2
    here = jnp.stack([h, k]).astype(jnp.int32)

    tile_row, tile_col = places // 32, places % 32
    far_h, far_k = (h - tile_row // 2) % 4, (k - tile_row) % 2
    far_x, far_y, far_z = (x - tile_col // 8) % 4, (y - tile_col // 2) % 4, (z - tile_col) % 2
    put_row = (far_k * 4 + far_h).astype(jnp.int32)
    put_col = (jnp.where(k == 0, far_x * 4 + far_y, far_y * 4 + far_x) * 2 + far_z).astype(jnp.int32)
    dense = spread(tile_values[0, 0], tile_count[0], put_row, put_col, 8, 32)

    source = jnp.stack([features, swap_z(features)])
    for turn in (0, 1):
        source = jnp.stack([source] + [move_xy(source, s, turn) for s in (1, 2, 3)])
    source = source.reshape(-1, feats)

    part = jnp.dot(dense, source, preferred_element_type=F32).reshape(2, 4, size, feats)
    half = part[0] + swap_k(part[1].astype(BF)).astype(F32)
    sent = half.astype(BF)
    arrived = [move_h(sent[s], -s) for s in (1, 2, 3)]
    hidden_out, sent, gw = middle(here, half[0], arrived, weight, bias, cotangent)

    arrived = [move_h(sent[s], s) for s in (1, 2, 3)]
    target = jnp.concatenate([sent[0][:size]] + [v[:size] for v in arrived])
    gw = gw + sum(v[size:].astype(F32) for v in arrived)
    share = gw.shape[0] // 2
    arrived = swap_k(jnp.concatenate([target, pair(gw[share:])]))
    gw = gw[:share] + unpair(arrived[4 * size :])
    target = jnp.concatenate([target, arrived[: 4 * size]])
    gw = gw + swap_z(gw)

    grad = lax.dot_general(dense, target, (((0,), (0,)), ((), ())), preferred_element_type=F32)
    for turn in (1, 0):
        grad = grad.reshape(4, -1, feats)
        rows = grad.shape[1]
        low, extra = grad.astype(BF), gw.astype(BF)
        arrived = [move_xy(jnp.concatenate([low[s], extra]), -s, turn) for s in (1, 2, 3)]
        grad = grad[0] + sum(v[:rows].astype(F32) for v in arrived)
        one, two, three = [v[rows:].astype(F32) for v in arrived]
        gw = (extra.astype(F32) + two) + (one + three)
    grad_features = (grad[:size] + swap_z(grad[size:].astype(BF)).astype(F32)).astype(BF)

    share = share * width // (width + feats)
    grad_bias = gw[share : share + width // feats].reshape(width)
    gw = gw[:share].astype(BF)
    gw = jnp.concatenate([gw, swap_h(gw, 1)])
    gw = jnp.concatenate([gw, swap_h(gw, 3)])
    grad_weight = settle(here, gw, swap_k(gw), feats, width)
    return (hidden_out, grad_features, grad_weight, grad_bias)


def solution(mesh):
    in_specs = (
        P(("row", "col"), None),
        P(),
        P(),
        P("row", "col", None, None, None),
        P("row", "col", None),
        P("row", "col"),
        P(("col", "row"), None),
    )
    out_specs = (P(("col", "row"), None), P(("row", "col"), None), P(), P())
    return jax.shard_map(local, mesh=mesh, in_specs=in_specs, out_specs=out_specs, check_vma=False)
```

```python
import jax
import jax.numpy as jnp
from jax import lax
from jax.experimental import pallas as pl
from jax.experimental.pallas import tpu as pltpu
from jax.sharding import PartitionSpec as P

BF, F32 = jnp.bfloat16, jnp.float32
VMEM = pltpu.VMEM


def mirror(i, count, inner, mask):
    digit = (i // inner) % count
    return i + ((digit ^ mask) - digit) * inner


def swap_xy(v, mask, turn):
    pairs = []
    for i in range(256):
        row, col = i // 32, i % 32
        pairs.append((i, row * 32 + mirror(col, 4, 2 if row % 2 == turn else 8, mask)))
    return lax.ppermute(v, ("row", "col"), pairs)


def swap_h(v, mask):
    return lax.ppermute(v, "row", [(i, mirror(i, 4, 2, mask)) for i in range(8)])


def swap_k(v):
    return lax.ppermute(v, "row", [(i, i ^ 1) for i in range(8)])


def swap_z(v):
    return lax.ppermute(v, "col", [(i, i ^ 1) for i in range(32)])


def pair(v):
    high = v.astype(BF)
    return jnp.concatenate([high, (v - high.astype(F32)).astype(BF)])


def unpair(v):
    rows = v.shape[0] // 2
    return v[:rows].astype(F32) + v[rows:].astype(F32)


def spread_kernel(count_ref, put_row, put_col, tiles_ref, dense_ref):
    size = tiles_ref.shape[1]
    dense_ref[...] = jnp.zeros_like(dense_ref)

    def place(slot, carry):
        rows = pl.ds(pl.multiple_of(put_row[slot] * size, size), size)
        cols = pl.ds(pl.multiple_of(put_col[slot] * size, size), size)
        dense_ref[rows, cols] = tiles_ref[slot]
        return carry

    lax.fori_loop(0, count_ref[0], place, 0)


def spread(tiles, count, put_row, put_col, rows, cols):
    slots, size, _ = tiles.shape
    smem = pl.BlockSpec(memory_space=pltpu.SMEM)
    return pl.pallas_call(
        spread_kernel,
        out_shape=jax.ShapeDtypeStruct((rows * size, cols * size), BF),
        in_specs=[smem, smem, smem, pl.BlockSpec(memory_space=VMEM)],
        out_specs=pl.BlockSpec(memory_space=VMEM),
        compiler_params=pltpu.CompilerParams(vmem_limit_bytes=32 * 2**20),
        cost_estimate=pl.CostEstimate(
            flops=0, bytes_accessed=2 * size * size * (slots + rows * cols), transcendentals=0
        ),
        name="spread",
    )(count, put_row, put_col, tiles)


def middle_kernel(place, own, in1, in2, in3, weight, bias, cot, hidden_ref, sent_ref, gw_ref, whole):
    agg = own[...] + in1[...].astype(F32) + in2[...].astype(F32) + in3[...].astype(F32)
    high = agg.astype(BF)
    low = (agg - high.astype(F32)).astype(BF)
    w = weight[...]
    pre = (
        jnp.dot(high, w, preferred_element_type=F32)
        + jnp.dot(low, w, preferred_element_type=F32)
        + bias[...]
    )
    sig = jax.nn.sigmoid(pre)
    hidden_ref[...] = (pre * sig).astype(BF)
    dpre = (cot[...].astype(F32) * (sig + pre * sig * (1.0 - sig))).astype(BF)
    back = lax.dot_general(
        dpre, w, (((1,), (1,)), ((), ())), preferred_element_type=F32
    ).astype(BF)
    over_nodes = (((0,), (0,)), ((), ()))
    whole[...] = lax.dot_general(
        high, dpre, over_nodes, preferred_element_type=F32
    ) + lax.dot_general(low, dpre, over_nodes, preferred_element_type=F32)
    sums = jnp.sum(dpre.astype(F32), axis=0, keepdims=True)
    size, lanes = back.shape
    blocks = cot.shape[1] // lanes
    rows = whole.shape[0] // 8
    tail = jnp.concatenate(
        [sums[:, j * lanes : (j + 1) * lanes] for j in range(blocks)]
        + [jnp.zeros((16 - blocks, lanes), F32)]
    )
    last = 2 * blocks * rows
    gw_ref[last:, :] = tail
    for h in range(4):
        sent_ref[h, :size, :] = back
        sent_ref[h, size + last :, :] = tail.astype(BF)
        for k in range(2):
            at = ((place[0] ^ h) * 2 + (place[1] ^ k)) * rows
            at = pl.ds(pl.multiple_of(at, rows), rows)
            for j in range(blocks):
                piece = whole[at, j * lanes : (j + 1) * lanes]
                to = (k * blocks + j) * rows
                sent_ref[h, size + to : size + to + rows, :] = piece.astype(BF)
                if h == 0:
                    gw_ref[to : to + rows, :] = piece


def middle(place, own, arrived, weight, bias, cotangent):
    size, width = cotangent.shape
    feats = weight.shape[0]
    share = (feats // 4) * (width // feats) + 16
    vmem = pl.BlockSpec(memory_space=VMEM)
    return pl.pallas_call(
        middle_kernel,
        out_shape=(
            jax.ShapeDtypeStruct((size, width), BF),
            jax.ShapeDtypeStruct((4, size + share, feats), BF),
            jax.ShapeDtypeStruct((share, feats), F32),
        ),
        in_specs=[pl.BlockSpec(memory_space=pltpu.SMEM)] + [vmem] * 7,
        out_specs=(vmem, vmem, vmem),
        scratch_shapes=[VMEM((feats, width), F32)],
        compiler_params=pltpu.CompilerParams(vmem_limit_bytes=16 * 2**20),
        cost_estimate=pl.CostEstimate(
            flops=10 * size * feats * width, bytes_accessed=10 * size * width, transcendentals=size * width
        ),
        name="middle",
    )(place, own, *arrived, weight, bias[None, :], cotangent)


def settle_kernel(place, near, far, out_ref):
    lanes = near.shape[1]
    blocks = out_ref.shape[1] // lanes
    rows = near.shape[0] // 4 // blocks
    for k, part in ((0, near), (1, far)):
        for first in range(4):
            at = ((place[0] ^ first) * 2 + (place[1] ^ k)) * rows
            at = pl.ds(pl.multiple_of(at, rows), rows)
            for j in range(blocks):
                start = (first * blocks + j) * rows
                out_ref[at, j * lanes : (j + 1) * lanes] = part[start : start + rows, :].astype(F32)


def settle(place, near, far, feats, width):
    vmem = pl.BlockSpec(memory_space=VMEM)
    return pl.pallas_call(
        settle_kernel,
        out_shape=jax.ShapeDtypeStruct((feats, width), F32),
        in_specs=[pl.BlockSpec(memory_space=pltpu.SMEM), vmem, vmem],
        out_specs=vmem,
        compiler_params=pltpu.CompilerParams(vmem_limit_bytes=16 * 2**20),
        name="settle",
    )(place, near, far)


def local(features, weight, bias, tile_values, tile_index, tile_count, cotangent):
    size = features.shape[0]
    feats, width = weight.shape
    places = tile_index[0, 0]
    row, col = lax.axis_index("row"), lax.axis_index("col")
    h, k = row // 2, row % 2
    x, y, z = col // 8, (col // 2) % 4, col % 2
    here = jnp.stack([h, k]).astype(jnp.int32)

    tile_row, tile_col = places // 32, places % 32
    far_h, far_k = h ^ (tile_row // 2), k ^ (tile_row % 2)
    far_x, far_y, far_z = x ^ (tile_col // 8), y ^ ((tile_col // 2) % 4), z ^ (tile_col % 2)
    put_row = (far_k * 4 + far_h).astype(jnp.int32)
    first, second = jnp.where(k == 0, far_y, far_x), jnp.where(k == 0, far_x, far_y)
    put_col = (second * 8 + first * 2 + far_z).astype(jnp.int32)
    dense = spread(tile_values[0, 0], tile_count[0], put_row, put_col, 8, 32)

    source = jnp.stack([features, swap_z(features)])
    for turn in (0, 1):
        source = jnp.stack([source] + [swap_xy(source, bits, turn) for bits in (1, 2, 3)])
    source = source.reshape(-1, feats)

    part = jnp.dot(dense, source, preferred_element_type=F32).reshape(2, 4, size, feats)
    half = part[0] + swap_k(part[1].astype(BF)).astype(F32)
    sent = half.astype(BF)
    arrived = [swap_h(sent[s], s) for s in (1, 2, 3)]
    hidden_out, sent, gw = middle(here, half[0], arrived, weight, bias, cotangent)

    arrived = [swap_h(sent[s], s) for s in (1, 2, 3)]
    target = jnp.concatenate([sent[0][:size]] + [v[:size] for v in arrived])
    gw = gw + sum(v[size:].astype(F32) for v in arrived)
    share = (gw.shape[0] - 16) // 2
    own, other, sums = gw[:share], gw[share : 2 * share], gw[2 * share :]
    arrived = swap_k(jnp.concatenate([target, pair(jnp.concatenate([other, sums]))]))
    gw = jnp.concatenate([own, unpair(pair(sums))]) + unpair(arrived[4 * size :])
    target = jnp.concatenate([target, arrived[: 4 * size]])
    gw = gw + swap_z(gw)

    grad = lax.dot_general(dense, target, (((0,), (0,)), ((), ())), preferred_element_type=F32)
    for turn in (1, 0):
        grad = grad.reshape(4, -1, feats)
        rows = grad.shape[1]
        low, extra = grad.astype(BF), gw.astype(BF)
        arrived = [swap_xy(jnp.concatenate([low[s], extra]), s, turn) for s in (1, 2, 3)]
        grad = grad[0] + sum(v[:rows].astype(F32) for v in arrived)
        one, two, three = [v[rows:].astype(F32) for v in arrived]
        gw = (extra.astype(F32) + two) + (one + three)
    grad_features = (grad[:size] + swap_z(grad[size:].astype(BF)).astype(F32)).astype(BF)

    grad_bias = gw[share : share + width // feats].reshape(width)
    gw = gw[:share].astype(BF)
    gw = jnp.concatenate([gw] + [swap_h(gw, s) for s in (1, 2, 3)])
    grad_weight = settle(here, gw, swap_k(gw), feats, width)
    return (hidden_out, grad_features, grad_weight, grad_bias)


def solution(mesh):
    in_specs = (
        P(("row", "col"), None),
        P(),
        P(),
        P("row", "col", None, None, None),
        P("row", "col", None),
        P("row", "col"),
        P(("col", "row"), None),
    )
    out_specs = (P(("col", "row"), None), P(("row", "col"), None), P(), P())
    return jax.shard_map(local, mesh=mesh, in_specs=in_specs, out_specs=out_specs, check_vma=False)
```

```python
import jax
import jax.numpy as jnp
from jax import lax
from jax.experimental import pallas as pl
from jax.experimental.pallas import tpu as pltpu
from jax.sharding import PartitionSpec as P

BF, F32 = jnp.bfloat16, jnp.float32
VMEM = pltpu.VMEM


def mirror(i, count, inner, mask):
    digit = (i // inner) % count
    return i + ((digit ^ mask) - digit) * inner


def swap_xy(v, mask, turn):
    pairs = []
    for i in range(256):
        row, col = i // 32, i % 32
        pairs.append((i, row * 32 + mirror(col, 4, 2 if row % 2 == turn else 8, mask)))
    return lax.ppermute(v, ("row", "col"), pairs)


def swap_h(v, mask):
    return lax.ppermute(v, "row", [(i, mirror(i, 4, 2, mask)) for i in range(8)])


def swap_k(v):
    return lax.ppermute(v, "row", [(i, i ^ 1) for i in range(8)])


def swap_z(v):
    return lax.ppermute(v, "col", [(i, i ^ 1) for i in range(32)])


def pair(v):
    high = v.astype(BF)
    return jnp.concatenate([high, (v - high.astype(F32)).astype(BF)])


def unpair(v):
    rows = v.shape[0] // 2
    return v[:rows].astype(F32) + v[rows:].astype(F32)


def spread_kernel(count_ref, put_row, put_col, tiles_ref, dense_ref):
    size = tiles_ref.shape[1]
    dense_ref[...] = jnp.zeros_like(dense_ref)

    def place(slot, carry):
        rows = pl.ds(pl.multiple_of(put_row[slot] * size, size), size)
        cols = pl.ds(pl.multiple_of(put_col[slot] * size, size), size)
        dense_ref[rows, cols] = tiles_ref[slot]
        return carry

    lax.fori_loop(0, count_ref[0], place, 0)


def spread(tiles, count, put_row, put_col, rows, cols):
    slots, size, _ = tiles.shape
    smem = pl.BlockSpec(memory_space=pltpu.SMEM)
    return pl.pallas_call(
        spread_kernel,
        out_shape=jax.ShapeDtypeStruct((rows * size, cols * size), BF),
        in_specs=[smem, smem, smem, pl.BlockSpec(memory_space=VMEM)],
        out_specs=pl.BlockSpec(memory_space=VMEM),
        compiler_params=pltpu.CompilerParams(vmem_limit_bytes=32 * 2**20),
        cost_estimate=pl.CostEstimate(
            flops=0, bytes_accessed=2 * size * size * (slots + rows * cols), transcendentals=0
        ),
        name="spread",
    )(count, put_row, put_col, tiles)


def middle_kernel(place, own, in1, in2, in3, weight, bias, cot, hidden_ref, sent_ref, gw_ref, whole):
    agg = own[...] + in1[...].astype(F32) + in2[...].astype(F32) + in3[...].astype(F32)
    high = agg.astype(BF)
    low = (agg - high.astype(F32)).astype(BF)
    w = weight[...]
    pre = (
        jnp.dot(high, w, preferred_element_type=F32)
        + jnp.dot(low, w, preferred_element_type=F32)
        + bias[...]
    )
    sig = jax.nn.sigmoid(pre)
    hidden_ref[...] = (pre * sig).astype(BF)
    dpre = (cot[...].astype(F32) * (sig + pre * sig * (1.0 - sig))).astype(BF)
    back = lax.dot_general(
        dpre, w, (((1,), (1,)), ((), ())), preferred_element_type=F32
    ).astype(BF)
    over_nodes = (((0,), (0,)), ((), ()))
    whole[...] = lax.dot_general(
        high, dpre, over_nodes, preferred_element_type=F32
    ) + lax.dot_general(low, dpre, over_nodes, preferred_element_type=F32)
    sums = jnp.sum(dpre.astype(F32), axis=0, keepdims=True)
    size, lanes = back.shape
    blocks = cot.shape[1] // lanes
    rows = whole.shape[0] // 8
    tail = jnp.concatenate(
        [sums[:, j * lanes : (j + 1) * lanes] for j in range(blocks)]
        + [jnp.zeros((16 - blocks, lanes), F32)]
    )
    last = 2 * blocks * rows
    gw_ref[last:, :] = tail
    for h in range(4):
        sent_ref[h, :size, :] = back
        sent_ref[h, size + last :, :] = tail.astype(BF)
        for k in range(2):
            at = ((place[0] ^ h) * 2 + (place[1] ^ k)) * rows
            at = pl.ds(pl.multiple_of(at, rows), rows)
            for j in range(blocks):
                piece = whole[at, j * lanes : (j + 1) * lanes]
                to = (k * blocks + j) * rows
                sent_ref[h, size + to : size + to + rows, :] = piece.astype(BF)
                if h == 0:
                    gw_ref[to : to + rows, :] = piece


def middle(place, own, arrived, weight, bias, cotangent):
    size, width = cotangent.shape
    feats = weight.shape[0]
    share = (feats // 4) * (width // feats) + 16
    vmem = pl.BlockSpec(memory_space=VMEM)
    return pl.pallas_call(
        middle_kernel,
        out_shape=(
            jax.ShapeDtypeStruct((size, width), BF),
            jax.ShapeDtypeStruct((4, size + share, feats), BF),
            jax.ShapeDtypeStruct((share, feats), F32),
        ),
        in_specs=[pl.BlockSpec(memory_space=pltpu.SMEM)] + [vmem] * 7,
        out_specs=(vmem, vmem, vmem),
        scratch_shapes=[VMEM((feats, width), F32)],
        compiler_params=pltpu.CompilerParams(vmem_limit_bytes=16 * 2**20),
        cost_estimate=pl.CostEstimate(
            flops=10 * size * feats * width, bytes_accessed=10 * size * width, transcendentals=size * width
        ),
        name="middle",
    )(place, own, *arrived, weight, bias[None, :], cotangent)


def settle_kernel(place, own, one, two, three, far, out_ref, bias_ref):
    lanes = own.shape[1]
    blocks = out_ref.shape[1] // lanes
    rows = out_ref.shape[0] // 8
    share = blocks * rows
    parts = [(0, bits, ref, 0) for bits, ref in enumerate((own, one, two, three))]
    parts += [(1, bits, far, bits * share) for bits in range(4)]
    for k, bits, ref, start in parts:
        at = pl.ds(pl.multiple_of(((place[0] ^ bits) * 2 + (place[1] ^ k)) * rows, rows), rows)
        for j in range(blocks):
            piece = ref[start + j * rows : start + (j + 1) * rows, :]
            out_ref[at, j * lanes : (j + 1) * lanes] = piece.astype(F32)
    mine, other = own[share:, :].astype(F32), far[4 * share :, :].astype(F32)
    sums = jnp.where(place[1] == 0, mine, other)
    for j in range(blocks):
        bias_ref[:, j * lanes : (j + 1) * lanes] = sums[j : j + 1, :] + sums[8 + j : 9 + j, :]


def settle(place, own, arrived, far, feats, width):
    vmem = pl.BlockSpec(memory_space=VMEM)
    return pl.pallas_call(
        settle_kernel,
        out_shape=(
            jax.ShapeDtypeStruct((feats, width), F32),
            jax.ShapeDtypeStruct((1, width), F32),
        ),
        in_specs=[pl.BlockSpec(memory_space=pltpu.SMEM)] + [vmem] * 5,
        out_specs=(vmem, vmem),
        compiler_params=pltpu.CompilerParams(vmem_limit_bytes=16 * 2**20),
        name="settle",
    )(place, own, *arrived, far)


def near_kernel(v_ref, out_ref):
    out_ref[...] = v_ref[...]


def near_copy(v):
    vmem = pl.BlockSpec(memory_space=VMEM)
    return pl.pallas_call(
        near_kernel,
        out_shape=jax.ShapeDtypeStruct(v.shape, v.dtype),
        in_specs=[vmem],
        out_specs=vmem,
        compiler_params=pltpu.CompilerParams(vmem_limit_bytes=4 * 2**20),
        cost_estimate=pl.CostEstimate(flops=0, bytes_accessed=4 * v.size, transcendentals=0),
        name="near_copy",
    )(v)


def local(features, weight, bias, tile_values, tile_index, tile_count, cotangent):
    size = features.shape[0]
    feats, width = weight.shape
    places = tile_index[0, 0]
    row, col = lax.axis_index("row"), lax.axis_index("col")
    h, k = row // 2, row % 2
    x, y, z = col // 8, (col // 2) % 4, col % 2
    here = jnp.stack([h, k]).astype(jnp.int32)

    tile_row, tile_col = places // 32, places % 32
    far_h, far_k = h ^ (tile_row // 2), k ^ (tile_row % 2)
    far_x, far_y, far_z = x ^ (tile_col // 8), y ^ ((tile_col // 2) % 4), z ^ (tile_col % 2)
    put_row = (far_k * 4 + far_h).astype(jnp.int32)
    first, second = jnp.where(k == 0, far_y, far_x), jnp.where(k == 0, far_x, far_y)
    put_col = (second * 8 + first * 2 + far_z).astype(jnp.int32)
    dense = spread(tile_values[0, 0], tile_count[0], put_row, put_col, 8, 32)

    source = jnp.stack([near_copy(features), swap_z(features)])
    for turn in (0, 1):
        source = jnp.stack([source] + [swap_xy(source, bits, turn) for bits in (1, 2, 3)])
    source = source.reshape(-1, feats)

    part = jnp.dot(dense, source, preferred_element_type=F32).reshape(2, 4, size, feats)
    half = part[0] + swap_k(part[1].astype(BF)).astype(F32)
    sent = half.astype(BF)
    arrived = [swap_h(sent[s], s) for s in (1, 2, 3)]
    hidden_out, sent, gw = middle(here, half[0], arrived, weight, bias, cotangent)

    arrived = [swap_h(sent[s], s) for s in (1, 2, 3)]
    target = jnp.concatenate([sent[0][:size]] + [v[:size] for v in arrived])
    gw = gw + sum(v[size:].astype(F32) for v in arrived)
    share = (gw.shape[0] - 16) // 2
    own, other, sums = gw[:share], gw[share : 2 * share], gw[2 * share :]
    arrived = swap_k(jnp.concatenate([target, pair(jnp.concatenate([other, sums]))]))
    gw = jnp.concatenate([own, unpair(pair(sums))]) + unpair(arrived[4 * size :])
    target = jnp.concatenate([target, arrived[: 4 * size]])
    gw = gw + swap_z(gw)

    grad = lax.dot_general(dense, target, (((0,), (0,)), ((), ())), preferred_element_type=F32)
    for turn in (1, 0):
        grad = grad.reshape(4, -1, feats)
        rows = grad.shape[1]
        low, extra = grad.astype(BF), gw.astype(BF)
        arrived = [swap_xy(jnp.concatenate([low[s], extra]), s, turn) for s in (1, 2, 3)]
        grad = grad[0] + sum(v[:rows].astype(F32) for v in arrived)
        one, two, three = [v[rows:].astype(F32) for v in arrived]
        gw = (extra.astype(F32) + two) + (one + three)
    grad_features = (grad[:size] + swap_z(grad[size:].astype(BF)).astype(F32)).astype(BF)

    sums = pair(gw[share : share + 8])
    gw = gw[:share].astype(BF)
    arrived = [swap_h(gw, s) for s in (1, 2, 3)]
    far = swap_k(jnp.concatenate([gw] + arrived + [sums]))
    own = jnp.concatenate([gw, sums])
    grad_weight, grad_bias = settle(here, own, arrived, far, feats, width)
    return (hidden_out, grad_features, grad_weight, grad_bias.reshape(width))


def solution(mesh):
    in_specs = (
        P(("row", "col"), None),
        P(),
        P(),
        P("row", "col", None, None, None),
        P("row", "col", None),
        P("row", "col"),
        P(("col", "row"), None),
    )
    out_specs = (P(("col", "row"), None), P(("row", "col"), None), P(), P())
    return jax.shard_map(local, mesh=mesh, in_specs=in_specs, out_specs=out_specs, check_vma=False)
```

```python
import jax
import jax.numpy as jnp
from jax import lax
from jax.experimental import pallas as pl
from jax.experimental.pallas import tpu as pltpu
from jax.sharding import PartitionSpec as P

BF, F32 = jnp.bfloat16, jnp.float32
VMEM = pltpu.VMEM


def mirror(i, count, inner, mask):
    digit = (i // inner) % count
    return i + ((digit ^ mask) - digit) * inner


def swap_xy(v, mask, turn):
    pairs = []
    for i in range(256):
        row, col = i // 32, i % 32
        pairs.append((i, row * 32 + mirror(col, 4, 2 if row % 2 == turn else 8, mask)))
    return lax.ppermute(v, ("row", "col"), pairs)


def swap_h(v, mask):
    return lax.ppermute(v, "row", [(i, mirror(i, 4, 2, mask)) for i in range(8)])


def swap_k(v):
    return lax.ppermute(v, "row", [(i, i ^ 1) for i in range(8)])


def swap_z(v):
    return lax.ppermute(v, "col", [(i, i ^ 1) for i in range(32)])


def pair(v):
    high = v.astype(BF)
    return jnp.concatenate([high, (v - high.astype(F32)).astype(BF)])


def unpair(v):
    rows = v.shape[0] // 2
    return v[:rows].astype(F32) + v[rows:].astype(F32)


def spread_kernel(count_ref, put_row, put_col, tiles_ref, dense_ref):
    size = tiles_ref.shape[1]
    dense_ref[...] = jnp.zeros_like(dense_ref)

    def place(slot, carry):
        rows = pl.ds(pl.multiple_of(put_row[slot] * size, size), size)
        cols = pl.ds(pl.multiple_of(put_col[slot] * size, size), size)
        dense_ref[rows, cols] = tiles_ref[slot]
        return carry

    lax.fori_loop(0, count_ref[0], place, 0)


def spread(tiles, count, put_row, put_col, rows, cols):
    slots, size, _ = tiles.shape
    smem = pl.BlockSpec(memory_space=pltpu.SMEM)
    return pl.pallas_call(
        spread_kernel,
        out_shape=jax.ShapeDtypeStruct((rows * size, cols * size), BF),
        in_specs=[smem, smem, smem, pl.BlockSpec(memory_space=VMEM)],
        out_specs=pl.BlockSpec(memory_space=VMEM),
        compiler_params=pltpu.CompilerParams(vmem_limit_bytes=32 * 2**20),
        cost_estimate=pl.CostEstimate(
            flops=0, bytes_accessed=2 * size * size * (slots + rows * cols), transcendentals=0
        ),
        name="spread",
    )(count, put_row, put_col, tiles)


def middle_kernel(place, own, in1, in2, in3, weight, bias, cot, hidden_ref, sent_ref, gw_ref, whole):
    agg = own[...] + in1[...].astype(F32) + in2[...].astype(F32) + in3[...].astype(F32)
    high = agg.astype(BF)
    low = (agg - high.astype(F32)).astype(BF)
    w = weight[...]
    pre = (
        jnp.dot(high, w, preferred_element_type=F32)
        + jnp.dot(low, w, preferred_element_type=F32)
        + bias[...]
    )
    sig = jax.nn.sigmoid(pre)
    hidden_ref[...] = (pre * sig).astype(BF)
    dpre = (cot[...].astype(F32) * (sig + pre * sig * (1.0 - sig))).astype(BF)
    back = lax.dot_general(
        dpre, w, (((1,), (1,)), ((), ())), preferred_element_type=F32
    ).astype(BF)
    over_nodes = (((0,), (0,)), ((), ()))
    whole[...] = lax.dot_general(
        high, dpre, over_nodes, preferred_element_type=F32
    ) + lax.dot_general(low, dpre, over_nodes, preferred_element_type=F32)
    sums = jnp.sum(dpre.astype(F32), axis=0, keepdims=True)
    size, lanes = back.shape
    blocks = cot.shape[1] // lanes
    rows = whole.shape[0] // 8
    tail = jnp.concatenate(
        [sums[:, j * lanes : (j + 1) * lanes] for j in range(blocks)]
        + [jnp.zeros((16 - blocks, lanes), F32)]
    )
    last = 2 * blocks * rows
    gw_ref[last:, :] = tail
    for h in range(4):
        sent_ref[h, :size, :] = back
        sent_ref[h, size + last :, :] = tail.astype(BF)
        for k in range(2):
            at = ((place[0] ^ h) * 2 + (place[1] ^ k)) * rows
            at = pl.ds(pl.multiple_of(at, rows), rows)
            for j in range(blocks):
                piece = whole[at, j * lanes : (j + 1) * lanes]
                to = (k * blocks + j) * rows
                sent_ref[h, size + to : size + to + rows, :] = piece.astype(BF)
                if h == 0:
                    gw_ref[to : to + rows, :] = piece


def middle(place, own, arrived, weight, bias, cotangent):
    size, width = cotangent.shape
    feats = weight.shape[0]
    share = (feats // 4) * (width // feats) + 16
    vmem = pl.BlockSpec(memory_space=VMEM)
    return pl.pallas_call(
        middle_kernel,
        out_shape=(
            jax.ShapeDtypeStruct((size, width), BF),
            jax.ShapeDtypeStruct((4, size + share, feats), BF),
            jax.ShapeDtypeStruct((share, feats), F32),
        ),
        in_specs=[pl.BlockSpec(memory_space=pltpu.SMEM)] + [vmem] * 7,
        out_specs=(vmem, vmem, vmem),
        scratch_shapes=[VMEM((feats, width), F32)],
        compiler_params=pltpu.CompilerParams(vmem_limit_bytes=16 * 2**20),
        cost_estimate=pl.CostEstimate(
            flops=10 * size * feats * width, bytes_accessed=10 * size * width, transcendentals=size * width
        ),
        name="middle",
    )(place, own, *arrived, weight, bias[None, :], cotangent)


def settle_kernel(place, own, one, two, three, far, out_ref, bias_ref):
    lanes = own.shape[1]
    blocks = out_ref.shape[1] // lanes
    rows = out_ref.shape[0] // 8
    share = blocks * rows
    parts = [(0, bits, ref, 0) for bits, ref in enumerate((own, one, two, three))]
    parts += [(1, bits, far, bits * share) for bits in range(4)]
    for k, bits, ref, start in parts:
        at = pl.ds(pl.multiple_of(((place[0] ^ bits) * 2 + (place[1] ^ k)) * rows, rows), rows)
        for j in range(blocks):
            piece = ref[start + j * rows : start + (j + 1) * rows, :]
            out_ref[at, j * lanes : (j + 1) * lanes] = piece.astype(F32)
    mine, other = own[share:, :].astype(F32), far[4 * share :, :].astype(F32)
    sums = jnp.where(place[1] == 0, mine, other)
    for j in range(blocks):
        bias_ref[:, j * lanes : (j + 1) * lanes] = sums[j : j + 1, :] + sums[8 + j : 9 + j, :]


def settle(place, own, arrived, far, feats, width):
    vmem = pl.BlockSpec(memory_space=VMEM)
    return pl.pallas_call(
        settle_kernel,
        out_shape=(
            jax.ShapeDtypeStruct((feats, width), F32),
            jax.ShapeDtypeStruct((1, width), F32),
        ),
        in_specs=[pl.BlockSpec(memory_space=pltpu.SMEM)] + [vmem] * 5,
        out_specs=(vmem, vmem),
        compiler_params=pltpu.CompilerParams(vmem_limit_bytes=16 * 2**20),
        name="settle",
    )(place, own, *arrived, far)


def near_kernel(v_ref, out_ref):
    out_ref[...] = v_ref[...]


def near_copy(v):
    vmem = pl.BlockSpec(memory_space=VMEM)
    return pl.pallas_call(
        near_kernel,
        out_shape=jax.ShapeDtypeStruct(v.shape, v.dtype),
        in_specs=[vmem],
        out_specs=vmem,
        compiler_params=pltpu.CompilerParams(vmem_limit_bytes=4 * 2**20),
        cost_estimate=pl.CostEstimate(flops=0, bytes_accessed=4 * v.size, transcendentals=0),
        name="near_copy",
    )(v)


def local(features, weight, bias, tile_values, tile_index, tile_count, cotangent):
    size = features.shape[0]
    feats, width = weight.shape
    places = tile_index[0, 0]
    row, col = lax.axis_index("row"), lax.axis_index("col")
    h, k = row // 2, row % 2
    x, y, z = col // 8, (col // 2) % 4, col % 2
    here = jnp.stack([h, k]).astype(jnp.int32)

    tile_row, tile_col = places // 32, places % 32
    far_h, far_k = h ^ (tile_row // 2), k ^ (tile_row % 2)
    far_x, far_y, far_z = x ^ (tile_col // 8), y ^ ((tile_col // 2) % 4), z ^ (tile_col % 2)
    put_row = (far_k * 4 + far_h).astype(jnp.int32)
    first, second = jnp.where(k == 0, far_y, far_x), jnp.where(k == 0, far_x, far_y)
    second = second ^ (second >> 1)
    put_col = (second * 8 + first * 2 + far_z).astype(jnp.int32)
    dense = spread(tile_values[0, 0], tile_count[0], put_row, put_col, 8, 32)

    source = jnp.stack([near_copy(features), swap_z(features)])
    for turn in (0, 1):
        source = jnp.stack([source] + [swap_xy(source, bits, turn) for bits in ((1, 3, 2) if turn else (1, 2, 3))])
    source = source.reshape(-1, feats)

    part = jnp.dot(dense, source, preferred_element_type=F32).reshape(2, 4, size, feats)
    half = part[0] + swap_k(part[1].astype(BF)).astype(F32)
    sent = half.astype(BF)
    arrived = [swap_h(sent[s], s) for s in (2, 3, 1)]
    hidden_out, sent, gw = middle(here, half[0], arrived, weight, bias, cotangent)

    one, three, two = [swap_h(sent[s], s) for s in (1, 3, 2)]
    arrived = [one, two, three]
    target = jnp.concatenate([sent[0][:size]] + [v[:size] for v in arrived])
    gw = gw + sum(v[size:].astype(F32) for v in arrived)
    share = (gw.shape[0] - 16) // 2
    own, other, sums = gw[:share], gw[share : 2 * share], gw[2 * share :]
    arrived = swap_k(jnp.concatenate([target, pair(jnp.concatenate([other, sums]))]))
    gw = jnp.concatenate([own, unpair(pair(sums))]) + unpair(arrived[4 * size :])
    target = jnp.concatenate([target, arrived[: 4 * size]])
    gw = gw + swap_z(gw)

    grad = lax.dot_general(dense, target, (((0,), (0,)), ((), ())), preferred_element_type=F32)
    for turn in (1, 0):
        grad = grad.reshape(4, -1, feats)
        rows = grad.shape[1]
        low, extra = grad.astype(BF), gw.astype(BF)
        order = (1, 3, 2) if turn else (1, 2, 3)
        arrived = [swap_xy(jnp.concatenate([low[i + 1], extra]), order[i], turn) for i in range(3)]
        grad = grad[0] + sum(v[:rows].astype(F32) for v in arrived)
        one, two, three = [arrived[order.index(bits)][rows:].astype(F32) for bits in (1, 2, 3)]
        gw = (extra.astype(F32) + two) + (one + three)
    grad_features = (grad[:size] + swap_z(grad[size:].astype(BF)).astype(F32)).astype(BF)

    sums = pair(gw[share : share + 8])
    gw = gw[:share].astype(BF)
    three, two, one = [swap_h(gw, s) for s in (3, 2, 1)]
    arrived = [one, two, three]
    far = swap_k(jnp.concatenate([gw] + arrived + [sums]))
    own = jnp.concatenate([gw, sums])
    grad_weight, grad_bias = settle(here, own, arrived, far, feats, width)
    return (hidden_out, grad_features, grad_weight, grad_bias.reshape(width))


def solution(mesh):
    in_specs = (
        P(("row", "col"), None),
        P(),
        P(),
        P("row", "col", None, None, None),
        P("row", "col", None),
        P("row", "col"),
        P(("col", "row"), None),
    )
    out_specs = (P(("col", "row"), None), P(("row", "col"), None), P(), P())
    return jax.shard_map(local, mesh=mesh, in_specs=in_specs, out_specs=out_specs, check_vma=False)
```

```python
import jax
import jax.numpy as jnp
from jax import lax
from jax.experimental import pallas as pl
from jax.experimental.pallas import tpu as pltpu
from jax.sharding import PartitionSpec as P

BF, F32 = jnp.bfloat16, jnp.float32
VMEM = pltpu.VMEM


def mirror(i, count, inner, mask):
    digit = (i // inner) % count
    return i + ((digit ^ mask) - digit) * inner


def swap_xy(v, mask, turn):
    pairs = []
    for i in range(256):
        row, col = i // 32, i % 32
        pairs.append((i, row * 32 + mirror(col, 4, 2 if row % 2 == turn else 8, mask)))
    return lax.ppermute(v, ("row", "col"), pairs)


def swap_h(v, mask):
    return lax.ppermute(v, "row", [(i, mirror(i, 4, 2, mask)) for i in range(8)])


def swap_k(v):
    return lax.ppermute(v, "row", [(i, i ^ 1) for i in range(8)])


def swap_z(v):
    return lax.ppermute(v, "col", [(i, i ^ 1) for i in range(32)])


def pair(v):
    high = v.astype(BF)
    return jnp.concatenate([high, (v - high.astype(F32)).astype(BF)])


def unpair(v):
    rows = v.shape[0] // 2
    return v[:rows].astype(F32) + v[rows:].astype(F32)


def spread_kernel(count_ref, put_row, put_col, tiles_ref, dense_ref):
    size = tiles_ref.shape[1]
    dense_ref[...] = jnp.zeros_like(dense_ref)

    def place(slot, carry):
        rows = pl.ds(pl.multiple_of(put_row[slot] * size, size), size)
        cols = pl.ds(pl.multiple_of(put_col[slot] * size, size), size)
        dense_ref[rows, cols] = tiles_ref[slot]
        return carry

    lax.fori_loop(0, count_ref[0], place, 0)


def spread(tiles, count, put_row, put_col, rows, cols):
    slots, size, _ = tiles.shape
    smem = pl.BlockSpec(memory_space=pltpu.SMEM)
    return pl.pallas_call(
        spread_kernel,
        out_shape=jax.ShapeDtypeStruct((rows * size, cols * size), BF),
        in_specs=[smem, smem, smem, pl.BlockSpec(memory_space=VMEM)],
        out_specs=pl.BlockSpec(memory_space=VMEM),
        compiler_params=pltpu.CompilerParams(vmem_limit_bytes=32 * 2**20),
        cost_estimate=pl.CostEstimate(
            flops=0, bytes_accessed=2 * size * size * (slots + rows * cols), transcendentals=0
        ),
        name="spread",
    )(count, put_row, put_col, tiles)


def middle_kernel(place, own, in1, in2, in3, weight, bias, cot, hidden_ref, sent_ref, gw_ref, whole):
    agg = own[...] + in1[...].astype(F32) + in2[...].astype(F32) + in3[...].astype(F32)
    high = agg.astype(BF)
    low = (agg - high.astype(F32)).astype(BF)
    w = weight[...]
    pre = (
        jnp.dot(high, w, preferred_element_type=F32)
        + jnp.dot(low, w, preferred_element_type=F32)
        + bias[...]
    )
    sig = jax.nn.sigmoid(pre)
    hidden_ref[...] = (pre * sig).astype(BF)
    dpre = (cot[...].astype(F32) * (sig + pre * sig * (1.0 - sig))).astype(BF)
    back = lax.dot_general(
        dpre, w, (((1,), (1,)), ((), ())), preferred_element_type=F32
    ).astype(BF)
    over_nodes = (((0,), (0,)), ((), ()))
    whole[...] = lax.dot_general(
        high, dpre, over_nodes, preferred_element_type=F32
    ) + lax.dot_general(low, dpre, over_nodes, preferred_element_type=F32)
    sums = jnp.sum(dpre.astype(F32), axis=0, keepdims=True)
    size, lanes = back.shape
    blocks = cot.shape[1] // lanes
    rows = whole.shape[0] // 8
    tail = jnp.concatenate(
        [sums[:, j * lanes : (j + 1) * lanes] for j in range(blocks)]
        + [jnp.zeros((16 - blocks, lanes), F32)]
    )
    last = 2 * blocks * rows
    gw_ref[last:, :] = tail
    for h in range(4):
        sent_ref[h, :size, :] = back
        sent_ref[h, size + last :, :] = tail.astype(BF)
        for k in range(2):
            at = ((place[0] ^ h) * 2 + (place[1] ^ k)) * rows
            at = pl.ds(pl.multiple_of(at, rows), rows)
            for j in range(blocks):
                piece = whole[at, j * lanes : (j + 1) * lanes]
                to = (k * blocks + j) * rows
                sent_ref[h, size + to : size + to + rows, :] = piece.astype(BF)
                if h == 0:
                    gw_ref[to : to + rows, :] = piece


def middle(place, own, arrived, weight, bias, cotangent):
    size, width = cotangent.shape
    feats = weight.shape[0]
    share = (feats // 4) * (width // feats) + 16
    vmem = pl.BlockSpec(memory_space=VMEM)
    return pl.pallas_call(
        middle_kernel,
        out_shape=(
            jax.ShapeDtypeStruct((size, width), BF),
            jax.ShapeDtypeStruct((4, size + share, feats), BF),
            jax.ShapeDtypeStruct((share, feats), F32),
        ),
        in_specs=[pl.BlockSpec(memory_space=pltpu.SMEM)] + [vmem] * 7,
        out_specs=(vmem, vmem, vmem),
        scratch_shapes=[VMEM((feats, width), F32)],
        compiler_params=pltpu.CompilerParams(vmem_limit_bytes=16 * 2**20),
        cost_estimate=pl.CostEstimate(
            flops=10 * size * feats * width, bytes_accessed=10 * size * width, transcendentals=size * width
        ),
        name="middle",
    )(place, own, *arrived, weight, bias[None, :], cotangent)


def settle_kernel(place, own, one, two, three, far, out_ref, bias_ref):
    lanes = own.shape[1]
    blocks = out_ref.shape[1] // lanes
    rows = out_ref.shape[0] // 8
    share = blocks * rows
    parts = [(0, bits, ref, 0) for bits, ref in enumerate((own, one, two, three))]
    parts += [(1, bits, far, bits * share) for bits in range(4)]
    for k, bits, ref, start in parts:
        at = pl.ds(pl.multiple_of(((place[0] ^ bits) * 2 + (place[1] ^ k)) * rows, rows), rows)
        for j in range(blocks):
            piece = ref[start + j * rows : start + (j + 1) * rows, :]
            out_ref[at, j * lanes : (j + 1) * lanes] = piece.astype(F32)
    mine, other = own[share:, :].astype(F32), far[4 * share :, :].astype(F32)
    sums = jnp.where(place[1] == 0, mine, other)
    for j in range(blocks):
        bias_ref[:, j * lanes : (j + 1) * lanes] = sums[j : j + 1, :] + sums[8 + j : 9 + j, :]


def settle(place, own, arrived, far, feats, width):
    vmem = pl.BlockSpec(memory_space=VMEM)
    return pl.pallas_call(
        settle_kernel,
        out_shape=(
            jax.ShapeDtypeStruct((feats, width), F32),
            jax.ShapeDtypeStruct((1, width), F32),
        ),
        in_specs=[pl.BlockSpec(memory_space=pltpu.SMEM)] + [vmem] * 5,
        out_specs=(vmem, vmem),
        compiler_params=pltpu.CompilerParams(vmem_limit_bytes=16 * 2**20),
        name="settle",
    )(place, own, *arrived, far)


def near_kernel(v_ref, out_ref):
    out_ref[...] = v_ref[...]


def near_copy(v):
    vmem = pl.BlockSpec(memory_space=VMEM)
    return pl.pallas_call(
        near_kernel,
        out_shape=jax.ShapeDtypeStruct(v.shape, v.dtype),
        in_specs=[vmem],
        out_specs=vmem,
        compiler_params=pltpu.CompilerParams(vmem_limit_bytes=4 * 2**20),
        cost_estimate=pl.CostEstimate(flops=0, bytes_accessed=4 * v.size, transcendentals=0),
        name="near_copy",
    )(v)


def local(features, weight, bias, tile_values, tile_index, tile_count, cotangent):
    size = features.shape[0]
    feats, width = weight.shape
    places = tile_index[0, 0]
    row, col = lax.axis_index("row"), lax.axis_index("col")
    h, k = row // 2, row % 2
    x, y, z = col // 8, (col // 2) % 4, col % 2
    here = jnp.stack([h, k]).astype(jnp.int32)

    tile_row, tile_col = places // 32, places % 32
    far_h, far_k = h ^ (tile_row // 2), k ^ (tile_row % 2)
    far_x, far_y, far_z = x ^ (tile_col // 8), y ^ ((tile_col // 2) % 4), z ^ (tile_col % 2)
    put_row = (far_k * 4 + far_h).astype(jnp.int32)
    first, second = jnp.where(k == 0, far_y, far_x), jnp.where(k == 0, far_x, far_y)
    first, second = first ^ (first >> 1), second ^ (second >> 1)
    put_col = (second * 8 + first * 2 + far_z).astype(jnp.int32)
    dense = spread(tile_values[0, 0], tile_count[0], put_row, put_col, 8, 32)

    source = jnp.stack([near_copy(features), swap_z(features)])
    for turn in (0, 1):
        source = jnp.stack([source] + [swap_xy(source, bits, turn) for bits in (1, 3, 2)])
    source = source.reshape(-1, feats)

    part = jnp.dot(dense, source, preferred_element_type=F32).reshape(2, 4, size, feats)
    half = part[0] + swap_k(part[1].astype(BF)).astype(F32)
    sent = half.astype(BF)
    arrived = [swap_h(sent[s], s) for s in (2, 3, 1)]
    hidden_out, sent, gw = middle(here, half[0], arrived, weight, bias, cotangent)

    one, three, two = [swap_h(sent[s], s) for s in (1, 3, 2)]
    arrived = [one, two, three]
    target = jnp.concatenate([sent[0][:size]] + [v[:size] for v in arrived])
    gw = gw + sum(v[size:].astype(F32) for v in arrived)
    share = (gw.shape[0] - 16) // 2
    own, other, sums = gw[:share], gw[share : 2 * share], gw[2 * share :]
    arrived = swap_k(jnp.concatenate([target, pair(jnp.concatenate([other, sums]))]))
    gw = jnp.concatenate([own, unpair(pair(sums))]) + unpair(arrived[4 * size :])
    target = jnp.concatenate([target, arrived[: 4 * size]])
    gw = gw + swap_z(gw)

    grad = lax.dot_general(dense, target, (((0,), (0,)), ((), ())), preferred_element_type=F32)
    for turn in (1, 0):
        grad = grad.reshape(4, -1, feats)
        rows = grad.shape[1]
        low, extra = grad.astype(BF), gw.astype(BF)
        order = (1, 3, 2)
        arrived = [swap_xy(jnp.concatenate([low[i + 1], extra]), order[i], turn) for i in range(3)]
        grad = grad[0] + sum(v[:rows].astype(F32) for v in arrived)
        one, two, three = [arrived[order.index(bits)][rows:].astype(F32) for bits in (1, 2, 3)]
        gw = (extra.astype(F32) + two) + (one + three)
    grad_features = (grad[:size] + swap_z(grad[size:].astype(BF)).astype(F32)).astype(BF)

    sums = pair(gw[share : share + 8])
    gw = gw[:share].astype(BF)
    three, two, one = [swap_h(gw, s) for s in (3, 2, 1)]
    arrived = [one, two, three]
    far = swap_k(jnp.concatenate([gw] + arrived + [sums]))
    own = jnp.concatenate([gw, sums])
    grad_weight, grad_bias = settle(here, own, arrived, far, feats, width)
    return (hidden_out, grad_features, grad_weight, grad_bias.reshape(width))


def solution(mesh):
    in_specs = (
        P(("row", "col"), None),
        P(),
        P(),
        P("row", "col", None, None, None),
        P("row", "col", None),
        P("row", "col"),
        P(("col", "row"), None),
    )
    out_specs = (P(("col", "row"), None), P(("row", "col"), None), P(), P())
    return jax.shard_map(local, mesh=mesh, in_specs=in_specs, out_specs=out_specs, check_vma=False)
```
